32 devices in a mesh: dp: 2 (over y), ctx: 4 (over z), fsdp: 4 (over x, core).
Axes of the slice: x: 2, y: 2, z: 4, core: 2. Of those that a mesh axis runs over, the one named last changes fastest.
Arguments:
- inputs: bfloat16 [2, 4096, 640], P('dp', ('ctx', 'fsdp')), may hold values from -6 to 6
- positions: int32 [2, 4096], P('dp', ('ctx', 'fsdp')), may hold values from 0 to 4095, as said below
- cotangent: bfloat16 [2, 4096, 640], P('dp', ('ctx', 'fsdp')), may hold values from -6 to 6
- w_query: bfloat16 [640, 1024], P('fsdp'), may hold values from -0.25 to 0.25
- w_key: bfloat16 [640, 256], P('fsdp'), may hold values from -0.25 to 0.25
- w_value: bfloat16 [640, 256], P('fsdp'), may hold values from -0.25 to 0.25
- w_out: bfloat16 [1024, 640], P('fsdp'), may hold values from -0.375 to 0.375
- w_gate: bfloat16 [640, 2048], P('fsdp'), may hold values from -0.25 to 0.25
- w_up: bfloat16 [640, 2048], P('fsdp'), may hold values from -0.25 to 0.25
- w_down: bfloat16 [2048, 640], P('fsdp'), may hold values from -0.125 to 0.125
- gain_attn_in: bfloat16 [640], P('fsdp'), may hold values from 0.25 to 1.75
- gain_attn_out: bfloat16 [640], P('fsdp'), may hold values from 0.25 to 1.75
- gain_ffn_in: bfloat16 [640], P('fsdp'), may hold values from 0.25 to 1.75
- gain_ffn_out: bfloat16 [640], P('fsdp'), may hold values from 0.25 to 1.75
- gain_query: bfloat16 [256], P('fsdp'), may hold values from 0.25 to 1.75
- gain_key: bfloat16 [256], P('fsdp'), may hold values from 0.25 to 1.75
Outputs:
- outputs: bfloat16 [2, 4096, 640], P('dp', ('ctx', 'fsdp'))
- input_grad: bfloat16 [2, 4096, 640], P('dp', ('ctx', 'fsdp'))
- grad_w_query: float32 [640, 1024], P('fsdp')
- grad_w_key: float32 [640, 256], P('fsdp')
- grad_w_value: float32 [640, 256], P('fsdp')
- grad_w_out: float32 [1024, 640], P('fsdp')
- grad_w_gate: float32 [640, 2048], P('fsdp')
- grad_w_up: float32 [640, 2048], P('fsdp')
- grad_w_down: float32 [2048, 640], P('fsdp')
- grad_gain_attn_in: float32 [640], P('fsdp')
- grad_gain_attn_out: float32 [640], P('fsdp')
- grad_gain_ffn_in: float32 [640], P('fsdp')
- grad_gain_ffn_out: float32 [640], P('fsdp')
- grad_gain_query: float32 [256], P('fsdp')
- grad_gain_key: float32 [256], P('fsdp')
The draws below stay inside these ranges and needn't reach their ends.
Inputs may be any that keep to these rules, and one draw needn't show every extreme that they name: In each sequence the positions are a permutation of 0 to 4095. Each device's 256 positions are two runs of 128 consecutive positions, the lower first, beginning at c * 128 and at (31 - c) * 128 for some c, each c once per sequence.
All inputs are finite; a program needn't handle non-finite values.
Results may differ from the reference program's by a relative error of at most 0.019.
Values may be sent and summed in bfloat16 or wider, within the bound.
A program may use at most 320 MiB of HBM per device.

```python
import math
import jax
import jax.numpy as jnp
import numpy as np
from jax import lax

D = 640
HEADS = 4
HEAD_DIM = 256
FF = 2048
TOK_DEV = 256
SEQ = 4096
SEQS = 2


def draw_positions(key, part):
    key = jax.random.fold_in(key, 11)
    run_length = TOK_DEV // 2
    runs = SEQ // run_length
    pairs = runs // 2
    sequences = []
    for index in range(SEQS):
        order = jax.random.permutation(jax.random.fold_in(key, index), pairs)
        starts = jnp.stack([order * run_length, (runs - 1 - order) * run_length], 1)
        places = starts[:, :, None] + jnp.arange(run_length, dtype=jnp.int32)[None, None, :]
        sequences.append(places.reshape(SEQ))
    return jnp.stack(sequences).astype(jnp.int32)


def level_of(own_key, shape, split, low, largest):
    loudness = 1.0
    for dim, parts in split:
        heights = jax.random.uniform(jax.random.fold_in(jax.random.fold_in(own_key, 6), dim), (parts,), jnp.float32, low / len(split), largest / len(split))
        loudness = loudness * jnp.repeat(jnp.exp(heights), shape[dim] // parts).reshape((-1,) + (1,) * (len(shape) - 1 - dim))
    return loudness


def normal_values(rng, dims, width, bound, cuts=(), kind=jnp.bfloat16):
    array = width * jax.random.normal(rng, dims, jnp.float32)
    if cuts:
        array = array * level_of(rng, dims, cuts, -0.22, 0.18)
    return jnp.clip(array, -bound, bound).astype(kind)


def setup_inputs(seed: int = 0) -> dict:
    streams_of = jax.random.split(jax.random.key(seed), 17)
    inputs = normal_values(streams_of[0], (SEQS, SEQ, D), 1.0, 6.0, ((0, 2), (1, 16)))
    positions = draw_positions(jax.random.fold_in(streams_of[16], 71), 0)
    cotangent = normal_values(streams_of[2], (SEQS, SEQ, D), 1.0, 6.0, ((0, 2), (1, 16)))
    w_query = normal_values(streams_of[3], (D, HEADS * HEAD_DIM), D ** -0.5, 0.25, ((0, 4),))
    w_key = normal_values(streams_of[4], (D, HEAD_DIM), D ** -0.5, 0.25, ((0, 4),))
    w_value = normal_values(streams_of[5], (D, HEAD_DIM), D ** -0.5, 0.25, ((0, 4),))
    w_out = normal_values(streams_of[6], (HEADS * HEAD_DIM, D), HEAD_DIM ** -0.5, 0.375, ((0, 4),))
    w_gate = normal_values(streams_of[7], (D, FF), D ** -0.5, 0.25, ((0, 4),))
    w_up = normal_values(streams_of[8], (D, FF), D ** -0.5, 0.25, ((0, 4),))
    w_down = normal_values(streams_of[9], (FF, D), FF ** -0.5, 0.125, ((0, 4),))
    gain_attn_in = jnp.clip(1.0 + 0.15 * jax.random.normal(streams_of[10], (D,), jnp.float32), 0.25, 1.75).astype(jnp.bfloat16)
    gain_attn_out = jnp.clip(1.0 + 0.15 * jax.random.normal(streams_of[11], (D,), jnp.float32), 0.25, 1.75).astype(jnp.bfloat16)
    gain_ffn_in = jnp.clip(1.0 + 0.15 * jax.random.normal(streams_of[12], (D,), jnp.float32), 0.25, 1.75).astype(jnp.bfloat16)
    gain_ffn_out = jnp.clip(1.0 + 0.15 * jax.random.normal(streams_of[13], (D,), jnp.float32), 0.25, 1.75).astype(jnp.bfloat16)
    gain_query = jnp.clip(1.0 + 0.15 * jax.random.normal(streams_of[14], (HEAD_DIM,), jnp.float32), 0.25, 1.75).astype(jnp.bfloat16)
    gain_key = jnp.clip(1.0 + 0.15 * jax.random.normal(streams_of[15], (HEAD_DIM,), jnp.float32), 0.25, 1.75).astype(jnp.bfloat16)
    return dict(inputs=inputs, positions=positions, cotangent=cotangent, w_query=w_query, w_key=w_key, w_value=w_value, w_out=w_out, w_gate=w_gate, w_up=w_up, w_down=w_down, gain_attn_in=gain_attn_in, gain_attn_out=gain_attn_out, gain_ffn_in=gain_ffn_in, gain_ffn_out=gain_ffn_out, gain_query=gain_query, gain_key=gain_key)


EPSILON = 1e-06
ROPE_BASE = 1000000.0
HIGHEST = lax.Precision.HIGHEST

@jax.custom_vjp
def low(v):
    return lax.optimization_barrier(v.astype(jnp.bfloat16)).astype(jnp.float32)

@jax.custom_vjp
def low_back(v):
    return v

def low_keep(v):
    return (low(v), None)

def low_pass(kept, grad):
    return (grad,)

def back_keep(v):
    return (v, None)

def back_low(kept, grad):
    return (low(grad),)
low.defvjp(low_keep, low_pass)
low_back.defvjp(back_keep, back_low)

def rms_norm(value, gain):
    return value * lax.rsqrt(lax.optimization_barrier(jnp.mean(value * value, -1, keepdims=True)) + EPSILON) * gain

def rope_tables(place, head_dim, length):
    half = head_dim // 2
    frequency = ROPE_BASE ** (-2.0 * np.arange(half) / head_dim)
    coarse = 128.0 * np.arange(length // 128 + 1)[:, None] * frequency[None, :]
    finer = 1.0 * np.arange(128)[:, None] * frequency[None, :]
    upper = place // 128
    lower = place % 128
    cos_upper = jnp.asarray(np.cos(coarse), jnp.float32)[upper]
    sin_upper = jnp.asarray(np.sin(coarse), jnp.float32)[upper]
    cos_lower = jnp.asarray(np.cos(finer), jnp.float32)[lower]
    sin_lower = jnp.asarray(np.sin(finer), jnp.float32)[lower]
    cosine = cos_upper * cos_lower - sin_upper * sin_lower
    sine = sin_upper * cos_lower + cos_upper * sin_lower
    return (cosine, sine)

def rotate(value, cosine, sine):
    half = value.shape[-1] // 2
    first = value[..., :half]
    second = value[..., half:]
    return jnp.concatenate([first * cosine - second * sine, second * cosine + first * sine], -1)

def attention(queries, keys, values, place):
    length = queries.shape[0]
    block = math.gcd(512, length)
    scale = HEAD_DIM ** (-0.5)

    def one_block(items):
        query_block, query_place = items
        scores = low_back(jnp.einsum('thd,ud->htu', query_block, keys, precision=HIGHEST) * scale)
        allowed = place[None, None, :] <= query_place[None, :, None]
        scores = jnp.where(allowed, scores, -1e+30)
        peak = lax.optimization_barrier(jnp.max(scores, -1, keepdims=True))
        weights = jnp.exp(scores - peak)
        probs = low(weights / lax.optimization_barrier(jnp.sum(weights, -1, keepdims=True)))
        return jnp.einsum('htu,ud->thd', probs, values, precision=HIGHEST)
    blocks = (queries.reshape(length // block, block, HEADS, HEAD_DIM), place.reshape(length // block, block))
    result = lax.map(jax.checkpoint(one_block), blocks)
    return result.reshape(length, HEADS, HEAD_DIM)

def layer(state, place, w_query, w_key, w_value, w_out, w_gate, w_up, w_down, gain_attn_in, gain_attn_out, gain_ffn_in, gain_ffn_out, gain_query, gain_key):
    length = state.shape[0]
    cosine, sine = rope_tables(place, HEAD_DIM, length)
    attn_in = low(rms_norm(state, gain_attn_in))
    query_proj = low_back(jnp.dot(attn_in, w_query, precision=HIGHEST)).reshape(length, HEADS, HEAD_DIM)
    key_proj = low_back(jnp.dot(attn_in, w_key, precision=HIGHEST))
    value_proj = low_back(jnp.dot(attn_in, w_value, precision=HIGHEST))
    queries = low(rotate(rms_norm(query_proj, gain_query), cosine[:, None, :], sine[:, None, :]))
    keys = low(rotate(rms_norm(key_proj, gain_key), cosine, sine))
    values = low(value_proj)
    attended = low(low_back(attention(queries, keys, values, place))).reshape(length, HEADS * HEAD_DIM)
    attn_out = low_back(jnp.dot(attended, w_out, precision=HIGHEST))
    middle = state + rms_norm(attn_out, gain_attn_out)
    ffn_in = low(rms_norm(middle, gain_ffn_in))
    gate = low_back(jnp.dot(ffn_in, w_gate, precision=HIGHEST))
    up_proj = low_back(jnp.dot(ffn_in, w_up, precision=HIGHEST))
    hidden = low(jax.nn.gelu(gate, approximate=True) * up_proj)
    down = low_back(jnp.dot(hidden, w_down, precision=HIGHEST))
    return middle + rms_norm(down, gain_ffn_out)

def reference(inputs, positions, cotangent, w_query, w_key, w_value, w_out, w_gate, w_up, w_down, gain_attn_in, gain_attn_out, gain_ffn_in, gain_ffn_out, gain_query, gain_key):
    weights = tuple((item.astype(jnp.float32) for item in (w_query, w_key, w_value, w_out, w_gate, w_up, w_down, gain_attn_in, gain_attn_out, gain_ffn_in, gain_ffn_out, gain_query, gain_key)))
    state = inputs.astype(jnp.float32)

    def forward(state, weights):
        return jnp.stack([layer(state[index], positions[index], *weights) for index in range(state.shape[0])])
    result, pull = jax.vjp(forward, state, weights)
    state_grad, grads = pull(cotangent.astype(jnp.float32))
    return (result.astype(jnp.bfloat16), state_grad.astype(jnp.bfloat16), grads[0], grads[1], grads[2], grads[3], grads[4], grads[5], grads[6], grads[7], grads[8], grads[9], grads[10], grads[11], grads[12])
```

```python
import functools

import jax
import jax.numpy as jnp
import numpy as np
from jax import lax
from jax.experimental import pallas as pl
from jax.experimental.pallas import tpu as pltpu
from jax.sharding import PartitionSpec as P

EPSILON = 1e-06
ROPE_BASE = 1000000.0
VMEM_BYTES = 48 * 1024 * 1024


def rms_norm(value, gain):
    return value * lax.rsqrt(jnp.mean(value * value, -1, keepdims=True) + EPSILON) * gain


def rms_back(value, gain, grad):
    inverse = lax.rsqrt(jnp.mean(value * value, -1, keepdims=True) + EPSILON)
    normal = value * inverse
    scaled = grad * gain
    gain_grad = jnp.sum((grad * normal).reshape(-1, value.shape[-1]), 0)
    value_grad = inverse * (scaled - normal * jnp.mean(scaled * normal, -1, keepdims=True))
    return (value_grad, gain_grad)


def rope_tables(run_ids, run_length, head_dim, length):
    half = head_dim // 2
    frequency = ROPE_BASE ** (-2.0 * np.arange(half) / head_dim)
    coarse = 1.0 * run_length * np.arange(length // run_length + 1)[:, None] * frequency[None, :]
    finer = 1.0 * np.arange(run_length)[:, None] * frequency[None, :]
    cos_upper = jnp.asarray(np.cos(coarse), jnp.float32)[run_ids][:, None, :]
    sin_upper = jnp.asarray(np.sin(coarse), jnp.float32)[run_ids][:, None, :]
    cos_lower = jnp.asarray(np.cos(finer), jnp.float32)[None]
    sin_lower = jnp.asarray(np.sin(finer), jnp.float32)[None]
    cosine = cos_upper * cos_lower - sin_upper * sin_lower
    sine = sin_upper * cos_lower + cos_upper * sin_lower
    return (cosine.reshape(-1, half), sine.reshape(-1, half))


def rotate(value, cosine, sine):
    half = value.shape[-1] // 2
    first = value[..., :half]
    second = value[..., half:]
    return jnp.concatenate([first * cosine - second * sine, second * cosine + first * sine], -1)


def contract_rows(left, right):
    return lax.dot_general(
        left, right, (((0,), (0,)), ((), ())), preferred_element_type=jnp.float32
    )


def times_transpose(left, right):
    return lax.dot_general(
        left, right, (((1,), (1,)), ((), ())), preferred_element_type=jnp.float32
    )


def causal(rows, columns, heads, first):
    token = lax.broadcasted_iota(jnp.int32, (rows, columns), 0) // heads
    key = lax.broadcasted_iota(jnp.int32, (rows, columns), 1) - first
    return key <= token


def forward_kernel(heads, run, ids, mine, query, pair, out, log_total, accum, total):
    step = pl.program_id(0)
    half = run * heads
    width = query.shape[1]

    @pl.when(step == 0)
    def clear():
        accum[...] = jnp.zeros_like(accum)
        total[...] = jnp.zeros_like(total)

    def visit(start, rows, columns, first):
        span = pl.ds(start, rows)
        weights = jnp.exp(times_transpose(query[span, :], pair[:columns, :width]))
        if first is not None:
            weights = jnp.where(causal(rows, columns, heads, first), weights, 0.0)
        folded = weights[:, :run]
        if columns > run:
            folded = folded + weights[:, run:]
        total[span, :] += folded
        accum[span, :] += jnp.dot(
            weights.astype(jnp.bfloat16),
            pair[:columns, width:],
            preferred_element_type=jnp.float32,
        )

    other = ids[step]
    own = mine[0]

    @pl.when(other < own)
    def earlier():
        visit(0, half, run, None)
        visit(half, half, run, None)

    @pl.when(other > own)
    def later():
        visit(half, half, 2 * run, None)

    @pl.when(other == own)
    def diagonal():
        visit(0, half, run, 0)
        visit(half, half, 2 * run, run)

    @pl.when(step == pl.num_programs(0) - 1)
    def finish():
        sums = jnp.sum(total[...], 1, keepdims=True)
        out[...] = accum[...] / sums
        log_total[...] = jnp.broadcast_to(jnp.log(sums), log_total.shape)


def backward_kernel(
    heads, run, ids, mine, query, pair, out_grad, out, log_total, query_grad, pair_grad, delta
):
    step = pl.program_id(0)
    half = run * heads
    width = query.shape[1]

    @pl.when(step == 0)
    def clear():
        query_grad[...] = jnp.zeros_like(query_grad)
        products = out_grad[...].astype(jnp.float32) * out[...]
        delta[...] = jnp.broadcast_to(jnp.sum(products, 1, keepdims=True), delta.shape)

    def visit(start, rows, columns, first):
        span = pl.ds(start, rows)
        keys = pair[:columns, :width]
        repeats = columns // run
        shift = jnp.concatenate([log_total[span, :]] * repeats, 1)
        less = jnp.concatenate([delta[span, :]] * repeats, 1)
        probs = jnp.exp(times_transpose(query[span, :], keys) - shift)
        if first is not None:
            probs = jnp.where(causal(rows, columns, heads, first), probs, 0.0)
        prob_grad = times_transpose(out_grad[span, :], pair[:columns, width:])
        score_grad = (probs * (prob_grad - less)).astype(jnp.bfloat16)
        query_grad[span, :] += jnp.dot(score_grad, keys, preferred_element_type=jnp.float32)
        key_part = contract_rows(score_grad, query[span, :])
        value_part = contract_rows(probs.astype(jnp.bfloat16), out_grad[span, :])
        return (key_part, value_part)

    def store(start, parts):
        rows = parts[0].shape[0]
        pair_grad[start : start + rows, :width] = parts[0].astype(jnp.bfloat16)
        pair_grad[start : start + rows, width:] = parts[1].astype(jnp.bfloat16)

    other = ids[step]
    own = mine[0]

    @pl.when(other < own)
    def earlier():
        store(0, visit(0, 2 * half, run, None))
        pair_grad[run:, :] = jnp.zeros((run, 2 * width), jnp.bfloat16)

    @pl.when(other > own)
    def later():
        store(0, visit(half, half, 2 * run, None))

    @pl.when(other == own)
    def diagonal():
        low = visit(0, half, run, 0)
        high = visit(half, half, 2 * run, run)
        store(0, (high[0][:run] + low[0], high[1][:run] + low[1]))
        store(run, (high[0][run:], high[1][run:]))


def attend(heads, run, ids, mine, query, pairs):
    rows, width = query.shape
    whole = lambda step, *unused: (0, 0)
    return pl.pallas_call(
        functools.partial(forward_kernel, heads, run),
        grid_spec=pltpu.PrefetchScalarGridSpec(
            num_scalar_prefetch=2,
            grid=(ids.shape[0],),
            in_specs=[
                pl.BlockSpec((rows, width), whole),
                pl.BlockSpec((2 * run, 2 * width), lambda step, *unused: (step, 0)),
            ],
            out_specs=[pl.BlockSpec((rows, width), whole), pl.BlockSpec((rows, run), whole)],
            scratch_shapes=[
                pltpu.VMEM((rows, width), jnp.float32),
                pltpu.VMEM((rows, run), jnp.float32),
            ],
        ),
        out_shape=[
            jax.ShapeDtypeStruct((rows, width), jnp.float32),
            jax.ShapeDtypeStruct((rows, run), jnp.float32),
        ],
        compiler_params=pltpu.CompilerParams(vmem_limit_bytes=VMEM_BYTES),
        name="attend",
    )(ids, mine, query, pairs)


def attend_back(heads, run, ids, mine, query, pairs, out_grad, out, log_total):
    rows, width = query.shape
    whole = lambda step, *unused: (0, 0)
    return pl.pallas_call(
        functools.partial(backward_kernel, heads, run),
        grid_spec=pltpu.PrefetchScalarGridSpec(
            num_scalar_prefetch=2,
            grid=(ids.shape[0],),
            in_specs=[
                pl.BlockSpec((rows, width), whole),
                pl.BlockSpec((2 * run, 2 * width), lambda step, *unused: (step, 0)),
                pl.BlockSpec((rows, width), whole),
                pl.BlockSpec((rows, width), whole),
                pl.BlockSpec((rows, run), whole),
            ],
            out_specs=[
                pl.BlockSpec((rows, width), whole),
                pl.BlockSpec((2 * run, 2 * width), lambda step, *unused: (step, 0)),
            ],
            scratch_shapes=[pltpu.VMEM((rows, run), jnp.float32)],
        ),
        out_shape=[
            jax.ShapeDtypeStruct((rows, width), jnp.float32),
            jax.ShapeDtypeStruct(pairs.shape, jnp.bfloat16),
        ],
        compiler_params=pltpu.CompilerParams(vmem_limit_bytes=VMEM_BYTES),
        name="attend_back",
    )(ids, mine, query, pairs, out_grad, out, log_total)


def per_device(
    inputs,
    positions,
    cotangent,
    w_query,
    w_key,
    w_value,
    w_out,
    w_gate,
    w_up,
    w_down,
    gain_attn_in,
    gain_attn_out,
    gain_ffn_in,
    gain_ffn_out,
    gain_query,
    gain_key,
):
    parts = lax.axis_size("fsdp")
    tokens, width = inputs.shape[1:]
    run = tokens // 2
    length = tokens * lax.axis_size("ctx") * parts
    head_dim = w_key.shape[1]
    query_dim = w_query.shape[1]
    heads = query_dim // head_dim
    hidden_dim = w_gate.shape[1]
    scale = head_dim ** (-0.5)

    gains = (gain_attn_in, gain_attn_out, gain_ffn_in, gain_ffn_out, gain_query, gain_key)
    cuts = np.cumsum([0] + [item.shape[0] for item in gains])
    gains_full = lax.all_gather(jnp.concatenate(gains), "fsdp", axis=0, tiled=False)
    qkv_full = lax.all_gather(
        jnp.concatenate([w_query, w_key, w_value], 1), "fsdp", axis=0, tiled=True
    )
    run_ids = positions[0].reshape(2, run)[:, 0] // run
    mine = run_ids[:1]
    ids = lax.all_gather(mine, ("ctx", "fsdp"), axis=0, tiled=True)
    out_full = lax.all_gather(w_out, "fsdp", axis=0, tiled=True)
    gate_up_full = lax.all_gather(
        jnp.concatenate([w_gate, w_up], 1), "fsdp", axis=0, tiled=True
    )
    down_full = lax.all_gather(w_down, "fsdp", axis=0, tiled=True)
    norm_attn_in, norm_attn_out, norm_ffn_in, norm_ffn_out, norm_query, norm_key = [
        gains_full[:, cuts[index] : cuts[index + 1]].reshape(-1).astype(jnp.float32)
        for index in range(len(gains))
    ]

    state = inputs[0].astype(jnp.float32)
    outer_grad = cotangent[0].astype(jnp.float32)
    cosine, sine = rope_tables(run_ids, run, head_dim, length)
    attn_in = rms_norm(state, norm_attn_in).astype(jnp.bfloat16)
    proj = jnp.dot(attn_in, qkv_full, preferred_element_type=jnp.float32)
    query_proj = proj[:, :query_dim].reshape(tokens, heads, head_dim)
    key_proj = proj[:, query_dim : query_dim + head_dim]
    keys = rotate(rms_norm(key_proj, norm_key), cosine, sine).astype(jnp.bfloat16)
    values = proj[:, query_dim + head_dim :].astype(jnp.bfloat16)
    pairs = lax.all_gather(
        jnp.concatenate([keys, values], 1), ("ctx", "fsdp"), axis=0, tiled=True
    )
    queries = rotate(rms_norm(query_proj, norm_query), cosine[:, None, :], sine[:, None, :])
    query_rows = (queries.astype(jnp.bfloat16) * scale).astype(jnp.bfloat16)
    query_rows = query_rows.reshape(tokens * heads, head_dim)
    out_rows, log_total = attend(heads, run, ids, mine, query_rows, pairs)
    attended = out_rows.astype(jnp.bfloat16).reshape(tokens, query_dim)

    attn_out = jnp.dot(attended, out_full, preferred_element_type=jnp.float32)
    middle = state + rms_norm(attn_out, norm_attn_out)
    ffn_in = rms_norm(middle, norm_ffn_in).astype(jnp.bfloat16)
    gate_up = jnp.dot(ffn_in, gate_up_full, preferred_element_type=jnp.float32)
    hidden_of = lambda both: (
        jax.nn.gelu(both[:, :hidden_dim], approximate=True) * both[:, hidden_dim:]
    )
    hidden_wide, pull = jax.vjp(hidden_of, gate_up)
    hidden = hidden_wide.astype(jnp.bfloat16)
    down = jnp.dot(hidden, down_full, preferred_element_type=jnp.float32)
    result = (middle + rms_norm(down, norm_ffn_out)).astype(jnp.bfloat16)

    def shard_sum(grad):
        part = lax.psum_scatter(
            grad.astype(jnp.bfloat16), "fsdp", scatter_dimension=0, tiled=True
        )
        return lax.psum(part, ("dp", "ctx")).astype(jnp.float32)

    down_grad, gain_ffn_out_grad = rms_back(down, norm_ffn_out, outer_grad)
    down_narrow = down_grad.astype(jnp.bfloat16)
    down_sum = shard_sum(contract_rows(hidden, down_narrow))
    gate_up_narrow = pull(times_transpose(down_narrow, down_full))[0].astype(jnp.bfloat16)
    gate_up_sum = shard_sum(contract_rows(ffn_in, gate_up_narrow))
    ffn_in_grad = times_transpose(gate_up_narrow, gate_up_full)
    middle_part, gain_ffn_in_grad = rms_back(middle, norm_ffn_in, ffn_in_grad)
    middle_grad = outer_grad + middle_part
    attn_grad, gain_attn_out_grad = rms_back(attn_out, norm_attn_out, middle_grad)
    attn_narrow = attn_grad.astype(jnp.bfloat16)
    out_sum = shard_sum(contract_rows(attended, attn_narrow))
    attended_grad = times_transpose(attn_narrow, out_full).astype(jnp.bfloat16)
    query_grad, pair_grads = attend_back(
        heads,
        run,
        ids,
        mine,
        query_rows,
        pairs,
        attended_grad.reshape(tokens * heads, head_dim),
        out_rows,
        log_total,
    )
    pair_grad = lax.psum_scatter(
        pair_grads, ("ctx", "fsdp"), scatter_dimension=0, tiled=True
    ).astype(jnp.float32)
    query_proj_grad, gain_query_grad = rms_back(
        query_proj,
        norm_query,
        rotate(
            (query_grad * scale).reshape(tokens, heads, head_dim),
            cosine[:, None, :],
            -sine[:, None, :],
        ),
    )
    key_proj_grad, gain_key_grad = rms_back(
        key_proj, norm_key, rotate(pair_grad[:, :head_dim], cosine, -sine)
    )
    qkv_narrow = jnp.concatenate(
        [
            query_proj_grad.reshape(tokens, query_dim).astype(jnp.bfloat16),
            key_proj_grad.astype(jnp.bfloat16),
            pair_grad[:, head_dim:].astype(jnp.bfloat16),
        ],
        1,
    )
    qkv_sum = shard_sum(contract_rows(attn_in, qkv_narrow))
    attn_in_grad = times_transpose(qkv_narrow, qkv_full)
    state_part, gain_attn_in_grad = rms_back(state, norm_attn_in, attn_in_grad)
    input_grad = (middle_grad + state_part).astype(jnp.bfloat16)
    gain_grads = jnp.concatenate(
        [
            item.reshape(parts, -1)
            for item in (
                gain_attn_in_grad,
                gain_attn_out_grad,
                gain_ffn_in_grad,
                gain_ffn_out_grad,
                gain_query_grad,
                gain_key_grad,
            )
        ],
        1,
    )
    gain_sums = lax.psum(gain_grads, ("dp", "ctx", "fsdp"))
    gain_sum = lax.dynamic_index_in_dim(gain_sums, lax.axis_index("fsdp"), 0, keepdims=False)
    return (
        result[None],
        input_grad[None],
        qkv_sum[:, :query_dim],
        qkv_sum[:, query_dim : query_dim + head_dim],
        qkv_sum[:, query_dim + head_dim :],
        out_sum,
        gate_up_sum[:, :hidden_dim],
        gate_up_sum[:, hidden_dim:],
        down_sum,
        *[gain_sum[cuts[index] : cuts[index + 1]] for index in range(len(gains))],
    )


def solution(mesh):
    in_specs = (
        P("dp", ("ctx", "fsdp"), None),
        P("dp", ("ctx", "fsdp")),
        P("dp", ("ctx", "fsdp"), None),
        P("fsdp", None),
        P("fsdp", None),
        P("fsdp", None),
        P("fsdp", None),
        P("fsdp", None),
        P("fsdp", None),
        P("fsdp", None),
        P("fsdp"),
        P("fsdp"),
        P("fsdp"),
        P("fsdp"),
        P("fsdp"),
        P("fsdp"),
    )
    out_specs = (
        P("dp", ("ctx", "fsdp"), None),
        P("dp", ("ctx", "fsdp"), None),
        P("fsdp", None),
        P("fsdp", None),
        P("fsdp", None),
        P("fsdp", None),
        P("fsdp", None),
        P("fsdp", None),
        P("fsdp", None),
        P("fsdp"),
        P("fsdp"),
        P("fsdp"),
        P("fsdp"),
        P("fsdp"),
        P("fsdp"),
    )
    return jax.shard_map(
        per_device, mesh=mesh, in_specs=in_specs, out_specs=out_specs, check_vma=False
    )
```
